32 devices in a mesh: sec: 2 (over y), row: 4 (over x, core), col: 4 (over z).
Axes of the slice: x: 2, y: 2, z: 4, core: 2. Of those that a mesh axis runs over, the one named last changes fastest.
Arguments:
- pairs: float32 [2, 2, 2048, 4096], P('sec', None, 'row', 'col'), may hold values from -0.75 to 0.75
Outputs:
- combined: float32 [2, 2, 2048, 4096], P('sec', None, 'row', 'col')
The draws below stay inside these ranges and needn't reach their ends.
All inputs are finite; a program needn't handle non-finite values.
Results may differ from the reference program's by a relative error of at most 0.0001.
Values sent between devices are 32-bit elements; how exact they have to be, the bound alone decides.
A program may use at most 128 MiB of HBM per device.

```python
import jax
import jax.numpy as jnp
from jax import lax

M = 2048
GROUPS = 2
CB = 512
N_SEC = 2
N_COL = 4


def shard_levels(key, extent, shards, least, top_value):
    factor_of, own = 1.0, jax.random.fold_in(key, 6)
    for axis_at, shards_of in shards:
        steps = jnp.exp(jax.random.uniform(jax.random.fold_in(own, axis_at), (shards_of,), jnp.float32, least / len(shards), top_value / len(shards)))
        factor_of = factor_of * jnp.repeat(steps, extent[axis_at] // shards_of).reshape([-1 if axis == axis_at else 1 for axis in range(len(extent))])
    return factor_of


def scatter_about(stream_key, shape, width, bound, cuts=(), dtype=jnp.bfloat16):
    array = jax.random.normal(stream_key, shape, jnp.float32) * width
    if len(cuts) > 0:
        array = shard_levels(stream_key, shape, cuts, -0.22, 0.18) * array
    return jnp.clip(array, min=-bound, max=bound).astype(dtype)


def setup_inputs(seed: int = 0) -> dict:
    splits = jax.random.split(jax.random.key(seed), 2)
    pairs = scatter_about(splits[0], (GROUPS, 2, M, 2 * M), ((2 * M) ** -0.25), 0.75, ((0, 2), (2, 4), (3, 4)), jnp.float32)
    return dict(pairs=pairs)


def real_dot(left, right):
    return jnp.dot(left, right, precision=lax.Precision.HIGHEST, preferred_element_type=jnp.float32)


def complex_times(a_re, a_im, b_re, b_im):
    return real_dot(a_re, b_re) - real_dot(a_im, b_im), real_dot(a_re, b_im) + real_dot(a_im, b_re)


def unpack(packed):
    shaped = packed.reshape(2, M, N_COL, 2, CB)
    return jnp.transpose(shaped, (0, 3, 1, 2, 4)).reshape(2, 2, M, M)


def pack_up(parts):
    shaped = parts.reshape(2, 2, M, N_COL, CB)
    return jnp.transpose(shaped, (0, 2, 3, 1, 4)).reshape(2, M, 2 * M)


def reference(pairs):
    results = []
    for couple in range(N_SEC // 2):
        first_pair = unpack(pairs[2 * couple])
        second_pair = unpack(pairs[2 * couple + 1])
        prod_re, prod_im = complex_times(first_pair[0, 0], first_pair[0, 1], second_pair[0, 0], second_pair[0, 1])
        left_re, left_im = complex_times(first_pair[1, 0], first_pair[1, 1], second_pair[0, 0], second_pair[0, 1])
        right_re, right_im = complex_times(first_pair[0, 0], first_pair[0, 1], second_pair[1, 0], second_pair[1, 1])
        result = jnp.stack([jnp.stack([prod_re, prod_im]), jnp.stack([left_re + right_re, left_im + right_im])])
        packed = pack_up(result)
        results.append(packed)
        results.append(packed)
    return jnp.stack(results)
```

```python
import functools

import jax
import jax.numpy as jnp
from jax import lax
from jax.experimental import pallas as pl
from jax.experimental.pallas import tpu as pltpu
from jax.sharding import PartitionSpec as P

MESH = pl.DeviceIdType.MESH
ROW_CHUNKS = 4
B_CHUNKS = 8


def split(x):
    hi = x.astype(jnp.bfloat16)
    lo = (x - hi.astype(jnp.float32)).astype(jnp.bfloat16)
    return hi, lo


def kernel(
    n_col, x_ref, o_ref, a_land, b_land, b_hi, b_lo, lhs, acc, out_v,
    a_recv, a_right, a_left, ya_send, b_recv, yb_send, b_send, out_sem,
):
    T, U = ROW_CHUNKS, B_CHUNKS
    rows, width = x_ref.shape[1], x_ref.shape[2]
    half = rows // 2
    mt = half // T
    ub = rows // U
    kw = width // 2
    tile = 256

    sec, row, col = lax.axis_index("sec"), lax.axis_index("row"), lax.axis_index("col")
    parity = lax.rem(sec, 2)
    partner = {"sec": sec + 1 - 2 * parity}
    row1 = row + 1 - 2 * lax.rem(row, 2)
    row2 = row + 2 - 4 * lax.rem(lax.div(row, 2), 2)
    row3 = row1 + row2 - row
    has_left, has_right = col > 0, col < n_col - 1

    def remote(src, dst, send, recv, device):
        return pltpu.make_async_remote_copy(
            src_ref=src, dst_ref=dst, send_sem=send, recv_sem=recv,
            device_id=device, device_id_type=MESH,
        )

    def a_slot(j, t):
        return a_land.at[j, t]

    def a_rows(t, base):
        return x_ref.at[:, pl.ds(base + t * mt, mt), :]

    def b_slot(who, u):
        return b_land.at[:, pl.ds(pl.multiple_of(who * rows + u * ub, ub), ub), :]

    def right_copy(j, t):
        return remote(a_slot(j, t), a_slot(j, t), a_right.at[j, t], a_recv.at[j, t], {"col": col + 1})

    def left_copy(j, t):
        return remote(a_slot(j, t), a_slot(j, t), a_left.at[j, t], a_recv.at[j, t], {"col": col - 1})

    def ya_copy(t):
        return remote(a_rows(t, half), a_slot(col, t), ya_send.at[t], a_recv.at[col, t], partner)

    def yb_copy(u):
        return remote(
            x_ref.at[:, pl.ds(u * ub, ub), :], b_slot(row, u), yb_send.at[u], b_recv.at[0, u], partner
        )

    def b_copy(kind, u):
        who = row2 if kind == 2 else row
        device = {"row": row2} if kind == 1 else {"row": row1}
        return remote(
            b_slot(who, u), b_slot(who, u), b_send.at[kind, u], b_recv.at[kind + 1, u], device
        )

    def b_wait(kind, who, u):
        pltpu.make_async_copy(b_slot(who, u), b_slot(who, u), b_recv.at[kind, u]).wait()

    def convert(who, u):
        step = 16

        @pl.loop(0, ub // step)
        def _(i):
            at = pl.ds(pl.multiple_of(who * rows + u * ub + i * step, step), step)
            hi, lo = split(b_land[:, at, :])
            b_hi[:, at, :] = hi
            b_lo[:, at, :] = lo

    def handle(j, t):
        pltpu.make_async_copy(a_slot(j, t), a_slot(j, t), a_recv.at[j, t]).wait()

        @pl.when(jnp.logical_and(j <= col, has_right))
        def _():
            right_copy(j, t).start()

        @pl.when(jnp.logical_and(j >= col, has_left))
        def _():
            left_copy(j, t).start()

    def a_tick(t, d):
        @pl.when(col >= d)
        def _():
            handle(col - d, t)

        @pl.when(col + d < n_col)
        def _():
            handle(col + d, t)

    def unit(j, t):
        for mat in range(2):
            for part in range(2):
                at = pl.ds((2 * mat + part) * mt, mt)
                hi, lo = split(a_land[j, t, mat, :, part * kw:(part + 1) * kw])
                lhs[at, 0:kw] = hi
                lhs[at, kw:2 * kw] = hi
                lhs[at, 2 * kw:3 * kw] = lo
        depth = pl.ds(pl.multiple_of(j * kw, kw), kw)

        @pl.loop(0, width // tile)
        def _(n):
            cols = pl.ds(pl.multiple_of(n * tile, tile), tile)
            rhs = []
            for mat in range(2):
                hi, lo = b_hi[mat, depth, cols], b_lo[mat, depth, cols]
                rhs.append(jnp.concatenate([hi, lo, hi], axis=0))
            acc[:, cols] += jnp.dot(lhs[...], rhs[0], preferred_element_type=jnp.float32)
            acc[2 * mt:4 * mt, cols] += jnp.dot(
                lhs[0:2 * mt, :], rhs[1], preferred_element_type=jnp.float32
            )

    def out_rows(t, base):
        return o_ref.at[:, pl.ds(pl.multiple_of(base + t * mt, mt), mt), :]

    def out_remote(t):
        return remote(
            out_v.at[t], out_rows(t, parity * half), out_sem.at[0, t], out_sem.at[1, t], partner
        )

    def out_local(t):
        return pltpu.make_async_copy(out_v.at[t], out_rows(t, parity * half), out_sem.at[2, t])

    def finish(t):
        for mat in range(2):
            p = acc[2 * mat * mt:(2 * mat + 1) * mt, :]
            q = acc[(2 * mat + 1) * mt:(2 * mat + 2) * mt, :]
            out_v[t, mat, :, 0:kw] = p[:, 0:kw] - q[:, kw:]
            out_v[t, mat, :, kw:] = p[:, kw:] + q[:, 0:kw]
        out_remote(t).start()
        out_local(t).start()

    barrier = pltpu.get_barrier_semaphore()
    for device in (partner, {"row": row1}, {"row": row2}):
        pl.semaphore_signal(barrier, inc=1, device_id=device, device_id_type=MESH)

    @pl.when(has_left)
    def _():
        pl.semaphore_signal(barrier, inc=1, device_id={"col": col - 1}, device_id_type=MESH)

    @pl.when(has_right)
    def _():
        pl.semaphore_signal(barrier, inc=1, device_id={"col": col + 1}, device_id_type=MESH)

    pl.semaphore_wait(barrier, 3 + has_left.astype(jnp.int32) + has_right.astype(jnp.int32))

    @pl.when(parity == 0)
    def _():
        for t in range(T):
            if t < 2:
                ya_copy(t).start()
            pltpu.make_async_copy(a_rows(t, 0), a_slot(col, t), a_recv.at[col, t]).start()

    @pl.when(parity == 1)
    def _():
        for u in range(U):
            if u < 2:
                yb_copy(u).start()
            pltpu.make_async_copy(
                x_ref.at[:, pl.ds(u * ub, ub), :], b_slot(row, u), b_recv.at[0, u]
            ).start()

    per_chunk = n_col - 1
    a_ticks = (T - 1) * per_chunk
    for tick in range(max(a_ticks, U + 2)):
        if tick == 0:
            handle(col, 0)
        if tick < U:
            b_wait(0, row, tick)
            b_copy(1, tick).start()
            b_copy(0, tick).start()
            convert(row, tick)
        if tick < a_ticks:
            t, d = tick // per_chunk, tick % per_chunk + 1
            a_tick(t, d)
            if d == max(per_chunk - 1, 1):
                handle(col, t + 1)
        if 1 <= tick < U + 1:
            b_wait(2, row2, tick - 1)
            b_copy(2, tick - 1).start()
            b_wait(1, row1, tick - 1)
            convert(row2, tick - 1)
            convert(row1, tick - 1)
        if 2 <= tick < U + 2:
            b_wait(3, row3, tick - 2)
            convert(row3, tick - 2)
        if tick + 2 < U:
            @pl.when(parity == 1)
            def _():
                yb_copy(tick).wait_send()
                yb_copy(tick + 2).start()
        if tick + 2 < T:
            @pl.when(parity == 0)
            def _():
                ya_copy(tick).wait_send()
                ya_copy(tick + 2).start()

    given = 0
    for t in range(T - 1):
        acc[...] = jnp.zeros_like(acc)

        @pl.loop(0, n_col)
        def _(j):
            unit(j, t)

        finish(t)
        due = per_chunk * (t + 1) // (T - 1) if t < T - 2 else per_chunk
        if t < T - 2:
            for d in range(given + 1, due + 1):
                a_tick(T - 1, d)
            given = due

    acc[...] = jnp.zeros_like(acc)
    unit(col, T - 1)

    @pl.loop(1, n_col)
    def _(d):
        for j, there in ((col - d, col >= d), (col + d, col + d < n_col)):
            @pl.when(there)
            def _():
                @pl.when(d > given)
                def _():
                    handle(j, T - 1)

                unit(j, T - 1)

    finish(T - 1)

    for t in range(T):
        out_local(t).wait()
        out_remote(t).wait_send()
        pltpu.make_async_copy(
            out_v.at[t], out_rows(t, (1 - parity) * half), out_sem.at[1, t]
        ).wait()

    for kind in range(3):
        for u in range(U):
            b_copy(kind, u).wait_send()

    @pl.when(parity == 0)
    def _():
        for t in range(max(T - 2, 0), T):
            ya_copy(t).wait_send()

    @pl.when(parity == 1)
    def _():
        for u in range(max(U - 2, 0), U):
            yb_copy(u).wait_send()

    @pl.loop(0, n_col)
    def _(j):
        @pl.when(jnp.logical_and(j <= col, has_right))
        def _():
            for t in range(T):
                right_copy(j, t).wait_send()

        @pl.when(jnp.logical_and(j >= col, has_left))
        def _():
            for t in range(T):
                left_copy(j, t).wait_send()


def shards(n_row, n_col, pairs):
    _, _, rows, width = pairs.shape
    T, U = ROW_CHUNKS, B_CHUNKS
    mt = rows // 2 // T
    dma = pltpu.SemaphoreType.DMA
    combined = pl.pallas_call(
        functools.partial(kernel, n_col),
        out_shape=jax.ShapeDtypeStruct((2, rows, width), jnp.float32),
        in_specs=[pl.BlockSpec(memory_space=pl.ANY)],
        out_specs=pl.BlockSpec(memory_space=pl.ANY),
        scratch_shapes=[
            pltpu.VMEM((n_col, T, 2, mt, width), jnp.float32),
            pltpu.VMEM((2, n_row * rows, width), jnp.float32),
            pltpu.VMEM((2, n_row * rows, width), jnp.bfloat16),
            pltpu.VMEM((2, n_row * rows, width), jnp.bfloat16),
            pltpu.VMEM((4 * mt, 3 * width // 2), jnp.bfloat16),
            pltpu.VMEM((4 * mt, width), jnp.float32),
            pltpu.VMEM((T, 2, mt, width), jnp.float32),
            dma((n_col, T)),
            dma((n_col, T)),
            dma((n_col, T)),
            dma((T,)),
            dma((4, U)),
            dma((U,)),
            dma((3, U)),
            dma((3, T)),
        ],
        compiler_params=pltpu.CompilerParams(
            collective_id=0, has_side_effects=True, vmem_limit_bytes=58 * 1024 * 1024
        ),
    )(pairs[0])
    return combined[None]


def solution(mesh):
    spec = P("sec", None, "row", "col")
    return jax.shard_map(
        functools.partial(shards, mesh.shape["row"], mesh.shape["col"]),
        mesh=mesh, in_specs=(spec,), out_specs=spec, check_vma=False,
    )
```

```python
import functools

import jax
import jax.numpy as jnp
from jax import lax
from jax.experimental import pallas as pl
from jax.experimental.pallas import tpu as pltpu
from jax.sharding import PartitionSpec as P

MESH = pl.DeviceIdType.MESH
ROW_CHUNKS = 4
B_CHUNKS = 8


def split(x):
    hi = x.astype(jnp.bfloat16)
    lo = (x - hi.astype(jnp.float32)).astype(jnp.bfloat16)
    return hi, lo


def kernel(
    n_col, x_ref, o_ref, a_land, b_land, b_hi, b_lo, lhs, acc, out_v,
    a_recv, a_right, a_left, ya_send, b_recv, yb_send, b_send, out_sem,
):
    T, U = ROW_CHUNKS, B_CHUNKS
    rows, width = x_ref.shape[1], x_ref.shape[2]
    half = rows // 2
    mt = half // T
    ub = rows // U
    kw = width // 2
    tile = 256

    sec, row, col = lax.axis_index("sec"), lax.axis_index("row"), lax.axis_index("col")
    parity = lax.rem(sec, 2)
    partner = {"sec": sec + 1 - 2 * parity}
    row1 = row + 1 - 2 * lax.rem(row, 2)
    row2 = row + 2 - 4 * lax.rem(lax.div(row, 2), 2)
    row3 = row1 + row2 - row
    has_left, has_right = col > 0, col < n_col - 1

    def remote(src, dst, send, recv, device):
        return pltpu.make_async_remote_copy(
            src_ref=src, dst_ref=dst, send_sem=send, recv_sem=recv,
            device_id=device, device_id_type=MESH,
        )

    def a_slot(j, t):
        return a_land.at[j, t]

    def a_rows(t, base):
        return x_ref.at[:, pl.ds(base + t * mt, mt), :]

    def b_slot(who, u):
        return b_land.at[:, pl.ds(pl.multiple_of(who * rows + u * ub, ub), ub), :]

    def right_copy(j, t):
        return remote(a_slot(j, t), a_slot(j, t), a_right.at[j, t], a_recv.at[j, t], {"col": col + 1})

    def left_copy(j, t):
        return remote(a_slot(j, t), a_slot(j, t), a_left.at[j, t], a_recv.at[j, t], {"col": col - 1})

    def ya_copy(t):
        return remote(a_rows(t, half), a_slot(col, t), ya_send.at[t], a_recv.at[col, t], partner)

    def yb_copy(u):
        return remote(
            x_ref.at[:, pl.ds(u * ub, ub), :], b_slot(row, u), yb_send.at[u], b_recv.at[0, u], partner
        )

    def b_copy(kind, u):
        who = row2 if kind == 2 else row
        device = {"row": row2} if kind == 1 else {"row": row1}
        return remote(
            b_slot(who, u), b_slot(who, u), b_send.at[kind, u], b_recv.at[kind + 1, u], device
        )

    def b_wait(kind, who, u):
        pltpu.make_async_copy(b_slot(who, u), b_slot(who, u), b_recv.at[kind, u]).wait()

    def convert(who, u):
        step = 16

        @pl.loop(0, ub // step)
        def _(i):
            at = pl.ds(pl.multiple_of(who * rows + u * ub + i * step, step), step)
            hi, lo = split(b_land[:, at, :])
            b_hi[:, at, :] = hi
            b_lo[:, at, :] = lo

    def handle(j, t):
        pltpu.make_async_copy(a_slot(j, t), a_slot(j, t), a_recv.at[j, t]).wait()

        @pl.when(jnp.logical_and(j <= col, has_right))
        def _():
            right_copy(j, t).start()

        @pl.when(jnp.logical_and(j >= col, has_left))
        def _():
            left_copy(j, t).start()

    def a_tick(t, d):
        @pl.when(col >= d)
        def _():
            handle(col - d, t)

        @pl.when(col + d < n_col)
        def _():
            handle(col + d, t)

    def unit(j, t, k0, depth):
        for mat in range(2):
            for part in range(2):
                at = pl.ds((2 * mat + part) * mt, mt)
                first = part * kw + k0
                hi, lo = split(a_land[j, t, mat, :, first:first + depth])
                lhs[at, 0:depth] = hi
                lhs[at, depth:2 * depth] = hi
                lhs[at, 2 * depth:3 * depth] = lo
        deep = pl.ds(pl.multiple_of(j * kw + k0, depth), depth)
        here = pl.ds(pl.multiple_of(t * mt, mt), mt)

        @pl.loop(0, width // tile)
        def _(n):
            cols = pl.ds(pl.multiple_of(n * tile, tile), tile)
            rhs = []
            for mat in range(2):
                hi, lo = b_hi[mat, deep, cols], b_lo[mat, deep, cols]
                rhs.append(jnp.concatenate([hi, lo, hi], axis=0))
            both = jnp.dot(lhs[:, 0:3 * depth], rhs[0], preferred_element_type=jnp.float32)
            cross = jnp.dot(
                lhs[0:2 * mt, 0:3 * depth], rhs[1], preferred_element_type=jnp.float32
            )
            acc[0:2, here, cols] += both[0:2 * mt].reshape(2, mt, tile)
            acc[2:4, here, cols] += (both[2 * mt:] + cross).reshape(2, mt, tile)

    def out_rows(t, base):
        return o_ref.at[:, pl.ds(pl.multiple_of(base + t * mt, mt), mt), :]

    def out_remote(t):
        return remote(
            out_v.at[t], out_rows(t, parity * half), out_sem.at[0, t], out_sem.at[1, t], partner
        )

    def out_local(t):
        return pltpu.make_async_copy(out_v.at[t], out_rows(t, parity * half), out_sem.at[2, t])

    def finish(t):
        here = pl.ds(pl.multiple_of(t * mt, mt), mt)
        for mat in range(2):
            p = acc[2 * mat, here, :]
            q = acc[2 * mat + 1, here, :]
            out_v[t, mat, :, 0:kw] = p[:, 0:kw] - q[:, kw:]
            out_v[t, mat, :, kw:] = p[:, kw:] + q[:, 0:kw]
        out_remote(t).start()
        out_local(t).start()

    barrier = pltpu.get_barrier_semaphore()
    for device in (partner, {"row": row1}, {"row": row2}):
        pl.semaphore_signal(barrier, inc=1, device_id=device, device_id_type=MESH)

    @pl.when(has_left)
    def _():
        pl.semaphore_signal(barrier, inc=1, device_id={"col": col - 1}, device_id_type=MESH)

    @pl.when(has_right)
    def _():
        pl.semaphore_signal(barrier, inc=1, device_id={"col": col + 1}, device_id_type=MESH)

    pl.semaphore_wait(barrier, 3 + has_left.astype(jnp.int32) + has_right.astype(jnp.int32))

    @pl.when(parity == 0)
    def _():
        for t in range(T):
            if t < 2:
                ya_copy(t).start()
            pltpu.make_async_copy(a_rows(t, 0), a_slot(col, t), a_recv.at[col, t]).start()

    @pl.when(parity == 1)
    def _():
        for u in range(U):
            if u < 3:
                yb_copy(u).start()
            pltpu.make_async_copy(
                x_ref.at[:, pl.ds(u * ub, ub), :], b_slot(row, u), b_recv.at[0, u]
            ).start()

    last = n_col - 1
    a_ticks = (last - 1) * T
    early = {U // 2 + 1: 0, U // 2 + 2: 1, 2 * T: 2} if kw == rows and n_col == 4 else {}

    @pl.when(parity == 0)
    def _():
        handle(col, 0)

    acc[...] = jnp.zeros_like(acc)
    for tick in range(max(a_ticks + 1, U + 2)):
        if tick < U:
            b_wait(0, row, tick)
            b_copy(1, tick).start()
            b_copy(0, tick).start()
        if tick < T:
            @pl.when(parity == 1)
            def _():
                handle(col, tick)
        if tick + 1 < T:
            @pl.when(parity == 0)
            def _():
                handle(col, tick + 1)
        if 1 <= tick < a_ticks + 1:
            a_tick((tick - 1) % T, (tick - 1) // T + 1)
        if 1 <= tick < U + 1:
            b_wait(2, row2, tick - 1)
            b_copy(2, tick - 1).start()
        if tick + 3 < U:
            @pl.when(parity == 1)
            def _():
                yb_copy(tick).wait_send()
                yb_copy(tick + 3).start()
        if tick + 2 < T:
            @pl.when(parity == 0)
            def _():
                ya_copy(tick).wait_send()
                ya_copy(tick + 2).start()
        if tick < U:
            convert(row, tick)
        if 1 <= tick < U + 1:
            b_wait(1, row1, tick - 1)
            convert(row1, tick - 1)
            convert(row2, tick - 1)
        if 2 <= tick < U + 2:
            b_wait(3, row3, tick - 2)
            convert(row3, tick - 2)
        if tick in early:
            dist = early[tick]

            @pl.loop(0, T * (2 if dist else 1))
            def _(i):
                j = col + dist * (1 - 2 * lax.div(i, T))

                @pl.when(jnp.logical_and(j >= 0, j < n_col))
                def _():
                    unit(j, lax.rem(i, T), 0, kw // 2)

    k0 = kw // 2 if early else 0

    @pl.loop(0, T)
    def _(t):
        @pl.loop(0, 2 * last - 1)
        def _(i):
            j = col + lax.div(i + 1, 2) * (1 - 2 * lax.rem(i, 2))

            @pl.when(jnp.logical_and(j >= 0, j < n_col))
            def _():
                unit(j, t, k0, kw - k0)

        @pl.when(jnp.logical_or(col == 0, col == last))
        def _():
            handle(last - col, t)
            unit(last - col, t, 0, kw)

        finish(t)

    for t in range(T):
        out_local(t).wait()
        out_remote(t).wait_send()
        pltpu.make_async_copy(
            out_v.at[t], out_rows(t, (1 - parity) * half), out_sem.at[1, t]
        ).wait()

    for kind in range(3):
        for u in range(U):
            b_copy(kind, u).wait_send()

    @pl.when(parity == 0)
    def _():
        for t in range(max(T - 2, 0), T):
            ya_copy(t).wait_send()

    @pl.when(parity == 1)
    def _():
        for u in range(max(U - 3, 0), U):
            yb_copy(u).wait_send()

    @pl.loop(0, n_col)
    def _(j):
        @pl.when(jnp.logical_and(j <= col, has_right))
        def _():
            for t in range(T):
                right_copy(j, t).wait_send()

        @pl.when(jnp.logical_and(j >= col, has_left))
        def _():
            for t in range(T):
                left_copy(j, t).wait_send()


def shards(n_row, n_col, pairs):
    _, _, rows, width = pairs.shape
    T, U = ROW_CHUNKS, B_CHUNKS
    mt = rows // 2 // T
    dma = pltpu.SemaphoreType.DMA
    combined = pl.pallas_call(
        functools.partial(kernel, n_col),
        out_shape=jax.ShapeDtypeStruct((2, rows, width), jnp.float32),
        in_specs=[pl.BlockSpec(memory_space=pl.ANY)],
        out_specs=pl.BlockSpec(memory_space=pl.ANY),
        scratch_shapes=[
            pltpu.VMEM((n_col, T, 2, mt, width), jnp.float32),
            pltpu.VMEM((2, n_row * rows, width), jnp.float32),
            pltpu.VMEM((2, n_row * rows, width), jnp.bfloat16),
            pltpu.VMEM((2, n_row * rows, width), jnp.bfloat16),
            pltpu.VMEM((4 * mt, 3 * width // 2), jnp.bfloat16),
            pltpu.VMEM((4, rows // 2, width), jnp.float32),
            pltpu.VMEM((T, 2, mt, width), jnp.float32),
            dma((n_col, T)),
            dma((n_col, T)),
            dma((n_col, T)),
            dma((T,)),
            dma((4, U)),
            dma((U,)),
            dma((3, U)),
            dma((3, T)),
        ],
        compiler_params=pltpu.CompilerParams(
            collective_id=0, has_side_effects=True, vmem_limit_bytes=58 * 1024 * 1024
        ),
    )(pairs[0])
    return combined[None]


def solution(mesh):
    spec = P("sec", None, "row", "col")
    return jax.shard_map(
        functools.partial(shards, mesh.shape["row"], mesh.shape["col"]),
        mesh=mesh, in_specs=(spec,), out_specs=spec, check_vma=False,
    )
```

```python
import functools

import jax
import jax.numpy as jnp
from jax import lax
from jax.experimental import pallas as pl
from jax.experimental.pallas import tpu as pltpu
from jax.sharding import PartitionSpec as P

MESH = pl.DeviceIdType.MESH
ROW_CHUNKS = 4
B_CHUNKS = 8


def split(x):
    hi = x.astype(jnp.bfloat16)
    lo = (x - hi.astype(jnp.float32)).astype(jnp.bfloat16)
    return hi, lo


def kernel(
    n_col, x_ref, o_ref, a_land, b_land, b_hi, b_lo, lhs, acc, out_v,
    a_recv, a_right, a_left, ya_send, b_recv, yb_send, b_send, out_sem,
):
    T, U = ROW_CHUNKS, B_CHUNKS
    rows, width = x_ref.shape[1], x_ref.shape[2]
    half = rows // 2
    mt = half // T
    ub = rows // U
    kw = width // 2
    tile = 256

    sec, row, col = lax.axis_index("sec"), lax.axis_index("row"), lax.axis_index("col")
    parity = lax.rem(sec, 2)
    partner = {"sec": sec + 1 - 2 * parity}
    row1 = row + 1 - 2 * lax.rem(row, 2)
    row2 = row + 2 - 4 * lax.rem(lax.div(row, 2), 2)
    row3 = row1 + row2 - row
    has_left, has_right = col > 0, col < n_col - 1

    def remote(src, dst, send, recv, device):
        return pltpu.make_async_remote_copy(
            src_ref=src, dst_ref=dst, send_sem=send, recv_sem=recv,
            device_id=device, device_id_type=MESH,
        )

    def a_slot(j, t):
        return a_land.at[j, t]

    def a_rows(t, base):
        return x_ref.at[:, pl.ds(base + t * mt, mt), :]

    def b_slot(who, u):
        return b_land.at[:, pl.ds(pl.multiple_of(who * rows + u * ub, ub), ub), :]

    def right_copy(j, t):
        return remote(a_slot(j, t), a_slot(j, t), a_right.at[j, t], a_recv.at[j, t], {"col": col + 1})

    def left_copy(j, t):
        return remote(a_slot(j, t), a_slot(j, t), a_left.at[j, t], a_recv.at[j, t], {"col": col - 1})

    def ya_copy(t):
        return remote(a_rows(t, half), a_slot(col, t), ya_send.at[t], a_recv.at[col, t], partner)

    def yb_copy(u):
        return remote(
            x_ref.at[:, pl.ds(u * ub, ub), :], b_slot(row, u), yb_send.at[u], b_recv.at[0, u], partner
        )

    def b_copy(kind, u):
        who = row2 if kind == 2 else row
        device = {"row": row2} if kind == 1 else {"row": row1}
        return remote(
            b_slot(who, u), b_slot(who, u), b_send.at[kind, u], b_recv.at[kind + 1, u], device
        )

    def b_wait(kind, who, u):
        pltpu.make_async_copy(b_slot(who, u), b_slot(who, u), b_recv.at[kind, u]).wait()

    def convert(who, u):
        step = 16

        @pl.loop(0, ub // step)
        def _(i):
            at = pl.ds(pl.multiple_of(who * rows + u * ub + i * step, step), step)
            hi, lo = split(b_land[:, at, :])
            b_hi[:, at, :] = hi
            b_lo[:, at, :] = lo

    def handle(j, t):
        pltpu.make_async_copy(a_slot(j, t), a_slot(j, t), a_recv.at[j, t]).wait()

        @pl.when(jnp.logical_and(j <= col, has_right))
        def _():
            right_copy(j, t).start()

        @pl.when(jnp.logical_and(j >= col, has_left))
        def _():
            left_copy(j, t).start()

    def a_tick(t, d):
        @pl.when(col >= d)
        def _():
            handle(col - d, t)

        @pl.when(col + d < n_col)
        def _():
            handle(col + d, t)

    def unit(j, t, n, k0, depth):
        m = n * mt
        for mat in range(2):
            for part in range(2):
                at = pl.ds((2 * mat + part) * m, m)
                first = part * kw + k0
                x = a_land[j, pl.ds(t, n), mat, :, first:first + depth]
                hi, lo = split(x.reshape(m, depth))
                lhs[at, 0:depth] = hi
                lhs[at, depth:2 * depth] = hi
                lhs[at, 2 * depth:3 * depth] = lo
        deep = pl.ds(pl.multiple_of(j * kw + k0, depth), depth)
        here = pl.ds(pl.multiple_of(t * mt, mt), m)

        @pl.loop(0, width // tile)
        def _(c):
            cols = pl.ds(pl.multiple_of(c * tile, tile), tile)
            rhs = []
            for mat in range(2):
                hi, lo = b_hi[mat, deep, cols], b_lo[mat, deep, cols]
                rhs.append(jnp.concatenate([hi, lo, hi], axis=0))
            both = jnp.dot(
                lhs[0:4 * m, 0:3 * depth], rhs[0], preferred_element_type=jnp.float32
            )
            acc[0:4, here, cols] += both.reshape(4, m, tile)
            cross = jnp.dot(
                lhs[0:2 * m, 0:3 * depth], rhs[1], preferred_element_type=jnp.float32
            )
            acc[2:4, here, cols] += cross.reshape(2, m, tile)

    def out_rows(t, base):
        return o_ref.at[:, pl.ds(pl.multiple_of(base + t * mt, mt), mt), :]

    def out_remote(t):
        return remote(
            out_v.at[t], out_rows(t, parity * half), out_sem.at[0, t], out_sem.at[1, t], partner
        )

    def out_local(t):
        return pltpu.make_async_copy(out_v.at[t], out_rows(t, parity * half), out_sem.at[2, t])

    def finish(t):
        here = pl.ds(pl.multiple_of(t * mt, mt), mt)
        for mat in range(2):
            p = acc[2 * mat, here, :]
            q = acc[2 * mat + 1, here, :]
            out_v[t, mat, :, 0:kw] = p[:, 0:kw] - q[:, kw:]
            out_v[t, mat, :, kw:] = p[:, kw:] + q[:, 0:kw]
        out_remote(t).start()
        out_local(t).start()

    barrier = pltpu.get_barrier_semaphore()
    for device in (partner, {"row": row1}, {"row": row2}):
        pl.semaphore_signal(barrier, inc=1, device_id=device, device_id_type=MESH)

    @pl.when(has_left)
    def _():
        pl.semaphore_signal(barrier, inc=1, device_id={"col": col - 1}, device_id_type=MESH)

    @pl.when(has_right)
    def _():
        pl.semaphore_signal(barrier, inc=1, device_id={"col": col + 1}, device_id_type=MESH)

    pl.semaphore_wait(barrier, 3 + has_left.astype(jnp.int32) + has_right.astype(jnp.int32))

    @pl.when(parity == 0)
    def _():
        for t in range(T):
            if t < 2:
                ya_copy(t).start()
            pltpu.make_async_copy(a_rows(t, 0), a_slot(col, t), a_recv.at[col, t]).start()

    @pl.when(parity == 1)
    def _():
        for u in range(U):
            if u < 3:
                yb_copy(u).start()
            pltpu.make_async_copy(
                x_ref.at[:, pl.ds(u * ub, ub), :], b_slot(row, u), b_recv.at[0, u]
            ).start()

    last = n_col - 1
    a_ticks = (last - 1) * T
    early = {5: (0, 0), 6: (-1, -1), 7: (1, 1), 8: (-2, 2)} if kw == rows and n_col == 4 else {}

    @pl.when(parity == 0)
    def _():
        handle(col, 0)

    acc[...] = jnp.zeros_like(acc)
    for tick in range(max(a_ticks + 1, U + 2)):
        if tick < U:
            b_wait(0, row, tick)
            b_copy(1, tick).start()
            b_copy(0, tick).start()
        if tick < T:
            @pl.when(parity == 1)
            def _():
                handle(col, tick)
        if tick + 1 < T:
            @pl.when(parity == 0)
            def _():
                handle(col, tick + 1)
        if 1 <= tick < a_ticks + 1:
            a_tick((tick - 1) % T, (tick - 1) // T + 1)
        if 1 <= tick < U + 1:
            b_wait(2, row2, tick - 1)
            b_copy(2, tick - 1).start()
        if tick + 3 < U:
            @pl.when(parity == 1)
            def _():
                yb_copy(tick).wait_send()
                yb_copy(tick + 3).start()
        if tick + 2 < T:
            @pl.when(parity == 0)
            def _():
                ya_copy(tick).wait_send()
                ya_copy(tick + 2).start()
        if tick < U:
            convert(row, tick)
        if 1 <= tick < U + 1:
            b_wait(1, row1, tick - 1)
            convert(row1, tick - 1)
            convert(row2, tick - 1)
        if 2 <= tick < U + 2:
            b_wait(3, row3, tick - 2)
            convert(row3, tick - 2)
        if tick in early:
            down, up = early[tick]
            j = jnp.where(col + down >= 0, col + down, col + up)

            @pl.when(jnp.logical_and(j >= 0, j < n_col))
            def _():
                @pl.loop(0, T // 2)
                def _(p):
                    unit(j, 2 * p, 2, 0, kw // 2)

    k0 = kw // 2 if early else 0

    @pl.loop(0, T // 2)
    def _(p):
        @pl.loop(0, 2 * last - 1)
        def _(i):
            j = col + lax.div(i + 1, 2) * (1 - 2 * lax.rem(i, 2))

            @pl.when(jnp.logical_and(j >= 0, j < n_col))
            def _():
                unit(j, 2 * p, 2, k0, kw - k0)

        @pl.loop(2 * p, 2 * p + 2)
        def _(t):
            @pl.when(jnp.logical_or(col == 0, col == last))
            def _():
                handle(last - col, t)
                unit(last - col, t, 1, 0, kw)

            finish(t)

    for t in range(T):
        out_local(t).wait()
        out_remote(t).wait_send()
        pltpu.make_async_copy(
            out_v.at[t], out_rows(t, (1 - parity) * half), out_sem.at[1, t]
        ).wait()

    for kind in range(3):
        for u in range(U):
            b_copy(kind, u).wait_send()

    @pl.when(parity == 0)
    def _():
        for t in range(max(T - 2, 0), T):
            ya_copy(t).wait_send()

    @pl.when(parity == 1)
    def _():
        for u in range(max(U - 3, 0), U):
            yb_copy(u).wait_send()

    @pl.loop(0, n_col)
    def _(j):
        @pl.when(jnp.logical_and(j <= col, has_right))
        def _():
            for t in range(T):
                right_copy(j, t).wait_send()

        @pl.when(jnp.logical_and(j >= col, has_left))
        def _():
            for t in range(T):
                left_copy(j, t).wait_send()


def shards(n_row, n_col, pairs):
    _, _, rows, width = pairs.shape
    T, U = ROW_CHUNKS, B_CHUNKS
    mt = rows // 2 // T
    dma = pltpu.SemaphoreType.DMA
    combined = pl.pallas_call(
        functools.partial(kernel, n_col),
        out_shape=jax.ShapeDtypeStruct((2, rows, width), jnp.float32),
        in_specs=[pl.BlockSpec(memory_space=pl.ANY)],
        out_specs=pl.BlockSpec(memory_space=pl.ANY),
        scratch_shapes=[
            pltpu.VMEM((n_col, T, 2, mt, width), jnp.float32),
            pltpu.VMEM((2, n_row * rows, width), jnp.float32),
            pltpu.VMEM((2, n_row * rows, width), jnp.bfloat16),
            pltpu.VMEM((2, n_row * rows, width), jnp.bfloat16),
            pltpu.VMEM((8 * mt, 3 * width // 2), jnp.bfloat16),
            pltpu.VMEM((4, rows // 2, width), jnp.float32),
            pltpu.VMEM((T, 2, mt, width), jnp.float32),
            dma((n_col, T)),
            dma((n_col, T)),
            dma((n_col, T)),
            dma((T,)),
            dma((4, U)),
            dma((U,)),
            dma((3, U)),
            dma((3, T)),
        ],
        compiler_params=pltpu.CompilerParams(
            collective_id=0, has_side_effects=True, vmem_limit_bytes=58 * 1024 * 1024
        ),
    )(pairs[0])
    return combined[None]


def solution(mesh):
    spec = P("sec", None, "row", "col")
    return jax.shard_map(
        functools.partial(shards, mesh.shape["row"], mesh.shape["col"]),
        mesh=mesh, in_specs=(spec,), out_specs=spec, check_vma=False,
    )
```

```python
import functools

import jax
import jax.numpy as jnp
from jax import lax
from jax.experimental import pallas as pl
from jax.experimental.pallas import tpu as pltpu
from jax.sharding import PartitionSpec as P

MESH = pl.DeviceIdType.MESH
ROW_CHUNKS = 4
LANES = 128


def split(x):
    hi = x.astype(jnp.bfloat16)
    lo = (x - hi.astype(jnp.float32)).astype(jnp.bfloat16)
    return hi, lo


def kernel(
    n_col, x_ref, o_ref, a_land, b_land, b_hi, b_lo, lhs, acc, out_v,
    a_recv, a_right, a_left, ya_send, b_recv, yb_send, b_send, out_sem,
):
    T = ROW_CHUNKS
    rows, width = x_ref.shape[1], x_ref.shape[2]
    U = width // LANES
    V = U // 2
    half = rows // 2
    mt = half // T
    kw = width // 2
    cw = LANES

    sec, row, col = lax.axis_index("sec"), lax.axis_index("row"), lax.axis_index("col")
    parity = lax.rem(sec, 2)
    partner = {"sec": sec + 1 - 2 * parity}
    row1 = row + 1 - 2 * lax.rem(row, 2)
    row2 = row + 2 - 4 * lax.rem(lax.div(row, 2), 2)
    row3 = row1 + row2 - row
    has_left, has_right = col > 0, col < n_col - 1

    def remote(src, dst, send, recv, device):
        return pltpu.make_async_remote_copy(
            src_ref=src, dst_ref=dst, send_sem=send, recv_sem=recv,
            device_id=device, device_id_type=MESH,
        )

    def a_slot(j, t):
        return a_land.at[j, t]

    def a_rows(t, base):
        return x_ref.at[:, pl.ds(base + t * mt, mt), :]

    def b_cols(u):
        return pl.ds((u % 2) * kw + (u // 2) * cw, cw)

    def b_slot(who, u):
        return b_land.at[:, pl.ds(pl.multiple_of(who * rows, rows), rows), b_cols(u)]

    def right_copy(j, t):
        return remote(a_slot(j, t), a_slot(j, t), a_right.at[j, t], a_recv.at[j, t], {"col": col + 1})

    def left_copy(j, t):
        return remote(a_slot(j, t), a_slot(j, t), a_left.at[j, t], a_recv.at[j, t], {"col": col - 1})

    def ya_copy(t):
        return remote(a_rows(t, half), a_slot(col, t), ya_send.at[t], a_recv.at[col, t], partner)

    def yb_copy(u):
        return remote(
            x_ref.at[:, :, b_cols(u)], b_slot(row, u), yb_send.at[u], b_recv.at[0, u], partner
        )

    def b_copy(kind, u):
        who = row2 if kind == 2 else row
        device = {"row": row2} if kind == 1 else {"row": row1}
        return remote(
            b_slot(who, u), b_slot(who, u), b_send.at[kind, u], b_recv.at[kind + 1, u], device
        )

    def b_wait(kind, who, u):
        pltpu.make_async_copy(b_slot(who, u), b_slot(who, u), b_recv.at[kind, u]).wait()

    def convert(who, u):
        step = 64
        part = u % 2

        @pl.loop(0, rows // step)
        def _(i):
            at = pl.ds(pl.multiple_of(who * rows + i * step, step), step)
            hi, lo = split(b_land[:, at, b_cols(u)])
            b_hi[u // 2, :, at, part * cw:(part + 1) * cw] = hi
            b_lo[u // 2, :, at, part * cw:(part + 1) * cw] = lo

    def handle(j, t):
        pltpu.make_async_copy(a_slot(j, t), a_slot(j, t), a_recv.at[j, t]).wait()

        @pl.when(jnp.logical_and(j <= col, has_right))
        def _():
            right_copy(j, t).start()

        @pl.when(jnp.logical_and(j >= col, has_left))
        def _():
            left_copy(j, t).start()

    def a_tick(t, d):
        @pl.when(col >= d)
        def _():
            handle(col - d, t)

        @pl.when(col + d < n_col)
        def _():
            handle(col + d, t)

    def load(j, t):
        for mat in range(2):
            for part in range(2):
                at = pl.ds((2 * mat + part) * mt, mt)
                hi, lo = split(a_land[j, t, mat, :, part * kw:(part + 1) * kw])
                lhs[at, 0:kw] = hi
                lhs[at, kw:2 * kw] = hi
                lhs[at, 2 * kw:3 * kw] = lo

    def add(j, v):
        deep = pl.ds(pl.multiple_of(j * kw, kw), kw)
        rhs = []
        for mat in range(2):
            hi, lo = b_hi[v, mat, deep, :], b_lo[v, mat, deep, :]
            rhs.append(jnp.concatenate([hi, lo, hi], axis=0))
        acc[v] += jnp.dot(lhs[...], rhs[0], preferred_element_type=jnp.float32)
        acc[v, 2 * mt:4 * mt, :] += jnp.dot(
            lhs[0:2 * mt, :], rhs[1], preferred_element_type=jnp.float32
        )

    def out_at(t, v, part, base):
        return o_ref.at[
            :, pl.ds(pl.multiple_of(base + t * mt, mt), mt),
            pl.ds(pl.multiple_of(part * kw + v * cw, cw), cw),
        ]

    def out_from(t, v, part):
        return out_v.at[t, :, :, pl.ds(pl.multiple_of(part * kw + v * cw, cw), cw)]

    def out_remote(t, v, part):
        return remote(
            out_from(t, v, part), out_at(t, v, part, parity * half),
            out_sem.at[0, t, v, part], out_sem.at[1, t, v, part], partner,
        )

    def out_local(t, v, part):
        return pltpu.make_async_copy(
            out_from(t, v, part), out_at(t, v, part, parity * half), out_sem.at[2, t, v, part]
        )

    def finish(t, v):
        for mat in range(2):
            p = acc[v, 2 * mat * mt:(2 * mat + 1) * mt, :]
            q = acc[v, (2 * mat + 1) * mt:(2 * mat + 2) * mt, :]
            re, im = (pl.ds(pl.multiple_of(part * kw + v * cw, cw), cw) for part in range(2))
            out_v[t, mat, :, re] = p[:, 0:cw] - q[:, cw:]
            out_v[t, mat, :, im] = p[:, cw:] + q[:, 0:cw]
        for part in range(2):
            out_remote(t, v, part).start()
            out_local(t, v, part).start()

    def clear(v0, v1):
        @pl.loop(v0, v1)
        def _(v):
            acc[v] = jnp.zeros((4 * mt, 2 * cw), jnp.float32)

    def sum_block(t, v0, v1, reach):
        @pl.loop(0, 2 * reach + 1)
        def _(i):
            j = col + lax.div(i + 1, 2) * (1 - 2 * lax.rem(i, 2))

            @pl.when(jnp.logical_and(j >= 0, j < n_col))
            def _():
                load(j, t)

                @pl.loop(v0, v1)
                def _(v):
                    add(j, v)

    def block(t0, t1, v0, v1):
        @pl.loop(t0, t1)
        def _(t):
            clear(v0, v1)
            sum_block(t, v0, v1, n_col - 1)

            @pl.loop(v0, v1)
            def _(v):
                finish(t, v)

    barrier = pltpu.get_barrier_semaphore()
    for device in (partner, {"row": row1}, {"row": row2}):
        pl.semaphore_signal(barrier, inc=1, device_id=device, device_id_type=MESH)

    @pl.when(has_left)
    def _():
        pl.semaphore_signal(barrier, inc=1, device_id={"col": col - 1}, device_id_type=MESH)

    @pl.when(has_right)
    def _():
        pl.semaphore_signal(barrier, inc=1, device_id={"col": col + 1}, device_id_type=MESH)

    pl.semaphore_wait(barrier, 3 + has_left.astype(jnp.int32) + has_right.astype(jnp.int32))

    @pl.when(parity == 0)
    def _():
        for t in range(T):
            if t < 2:
                ya_copy(t).start()
            pltpu.make_async_copy(a_rows(t, 0), a_slot(col, t), a_recv.at[col, t]).start()

    @pl.when(parity == 1)
    def _():
        for u in range(U):
            if u < 3:
                yb_copy(u).start()
            pltpu.make_async_copy(
                x_ref.at[:, :, b_cols(u)], b_slot(row, u), b_recv.at[0, u]
            ).start()

    last = n_col - 1
    a_ticks = T * last

    def own_b(u):
        b_wait(0, row, u)
        b_copy(1, u).start()
        b_copy(0, u).start()

    @pl.when(parity == 1)
    def _():
        own_b(0)

    done = [0] * T
    for tick in range(max(a_ticks + 1, U + 2)):
        if tick < U:
            @pl.when(parity == 0)
            def _():
                own_b(tick)
        if tick + 1 < U:
            @pl.when(parity == 1)
            def _():
                own_b(tick + 1)
        for t in range(T):
            if tick == max(t * last - max(last - 1, 1), 0):
                handle(col, t)
        if tick < a_ticks - 1:
            @pl.when(parity == 0)
            def _():
                a_tick(tick // last, tick % last + 1)
        if tick == a_ticks:
            a_tick(T - 1, last)
        if 1 <= tick < a_ticks:
            @pl.when(parity == 1)
            def _():
                a_tick((tick - 1) // last, (tick - 1) % last + 1)
        if 1 <= tick < U + 1:
            b_wait(2, row2, tick - 1)
            b_copy(2, tick - 1).start()
        if tick + 3 < U:
            @pl.when(parity == 1)
            def _():
                yb_copy(tick).wait_send()
                yb_copy(tick + 3).start()
        if tick + 2 < T:
            @pl.when(parity == 0)
            def _():
                ya_copy(tick).wait_send()
                ya_copy(tick + 2).start()
        if tick < U:
            convert(row, tick)
        if 1 <= tick < U + 1:
            b_wait(1, row1, tick - 1)
            convert(row1, tick - 1)
            convert(row2, tick - 1)
        if 2 <= tick < U + 2:
            b_wait(3, row3, tick - 2)
            convert(row3, tick - 2)
        have = min(max((tick - 1) // 2, 0), V)
        t0 = 0
        while t0 < T - 1:
            t1 = t0 + 1
            if tick >= (t0 + 1) * last and done[t0] < have:
                while t1 < T - 1 and tick >= (t1 + 1) * last and done[t1] == done[t0]:
                    t1 += 1
                block(t0, t1, done[t0], have)
                done[t0:t1] = [have] * (t1 - t0)
            t0 = t1
        if tick == max(a_ticks - 1, U + 1):
            clear(0, V)
            sum_block(T - 1, 0, V, last - 1)

    @pl.when(jnp.logical_or(col == 0, col == last))
    def _():
        load(last - col, T - 1)

    @pl.loop(0, V)
    def _(v):
        @pl.when(jnp.logical_or(col == 0, col == last))
        def _():
            add(last - col, v)

        finish(T - 1, v)

    @pl.loop(0, T)
    def _(t):
        @pl.loop(0, V)
        def _(v):
            for part in range(2):
                out_local(t, v, part).wait()
                out_remote(t, v, part).wait_send()
                pltpu.make_async_copy(
                    out_from(t, v, part), out_at(t, v, part, (1 - parity) * half),
                    out_sem.at[1, t, v, part],
                ).wait()

    for kind in range(3):
        for u in range(U):
            b_copy(kind, u).wait_send()

    @pl.when(parity == 0)
    def _():
        for t in range(max(T - 2, 0), T):
            ya_copy(t).wait_send()

    @pl.when(parity == 1)
    def _():
        for u in range(max(U - 3, 0), U):
            yb_copy(u).wait_send()

    @pl.loop(0, n_col)
    def _(j):
        @pl.when(jnp.logical_and(j <= col, has_right))
        def _():
            for t in range(T):
                right_copy(j, t).wait_send()

        @pl.when(jnp.logical_and(j >= col, has_left))
        def _():
            for t in range(T):
                left_copy(j, t).wait_send()


def shards(n_row, n_col, pairs):
    _, _, rows, width = pairs.shape
    T = ROW_CHUNKS
    U = width // LANES
    mt = rows // 2 // T
    dma = pltpu.SemaphoreType.DMA
    combined = pl.pallas_call(
        functools.partial(kernel, n_col),
        out_shape=jax.ShapeDtypeStruct((2, rows, width), jnp.float32),
        in_specs=[pl.BlockSpec(memory_space=pl.ANY)],
        out_specs=pl.BlockSpec(memory_space=pl.ANY),
        scratch_shapes=[
            pltpu.VMEM((n_col, T, 2, mt, width), jnp.float32),
            pltpu.VMEM((2, n_row * rows, width), jnp.float32),
            pltpu.VMEM((U // 2, 2, n_row * rows, 2 * LANES), jnp.bfloat16),
            pltpu.VMEM((U // 2, 2, n_row * rows, 2 * LANES), jnp.bfloat16),
            pltpu.VMEM((4 * mt, 3 * width // 2), jnp.bfloat16),
            pltpu.VMEM((U // 2, 4 * mt, 2 * LANES), jnp.float32),
            pltpu.VMEM((T, 2, mt, width), jnp.float32),
            dma((n_col, T)),
            dma((n_col, T)),
            dma((n_col, T)),
            dma((T,)),
            dma((4, U)),
            dma((U,)),
            dma((3, U)),
            dma((3, T, U // 2, 2)),
        ],
        compiler_params=pltpu.CompilerParams(
            collective_id=0, has_side_effects=True, vmem_limit_bytes=58 * 1024 * 1024
        ),
    )(pairs[0])
    return combined[None]


def solution(mesh):
    spec = P("sec", None, "row", "col")
    return jax.shard_map(
        functools.partial(shards, mesh.shape["row"], mesh.shape["col"]),
        mesh=mesh, in_specs=(spec,), out_specs=spec, check_vma=False,
    )
```

```python
import functools

import jax
import jax.numpy as jnp
from jax import lax
from jax.experimental import pallas as pl
from jax.experimental.pallas import tpu as pltpu
from jax.sharding import PartitionSpec as P

MESH = pl.DeviceIdType.MESH
ROW_CHUNKS = 4
LANES = 128


def split(x):
    hi = x.astype(jnp.bfloat16)
    lo = (x - hi.astype(jnp.float32)).astype(jnp.bfloat16)
    return hi, lo


def kernel(
    n_col, x_ref, o_ref, a_land, b_land, b_hi, b_lo, lhs, acc, out_v,
    a_recv, a_right, a_left, ya_send, b_recv, yb_send, b_send, out_sem,
):
    T = ROW_CHUNKS
    rows, width = x_ref.shape[1], x_ref.shape[2]
    U = width // LANES
    V = U // 2
    half = rows // 2
    mt = half // T
    kw = width // 2
    cw = LANES

    sec, row, col = lax.axis_index("sec"), lax.axis_index("row"), lax.axis_index("col")
    parity = lax.rem(sec, 2)
    partner = {"sec": sec + 1 - 2 * parity}
    row1 = row + 1 - 2 * lax.rem(row, 2)
    row2 = row + 2 - 4 * lax.rem(lax.div(row, 2), 2)
    row3 = row1 + row2 - row
    has_left, has_right = col > 0, col < n_col - 1

    def remote(src, dst, send, recv, device):
        return pltpu.make_async_remote_copy(
            src_ref=src, dst_ref=dst, send_sem=send, recv_sem=recv,
            device_id=device, device_id_type=MESH,
        )

    def a_slot(j, t):
        return a_land.at[j, t]

    def a_rows(t, base):
        return x_ref.at[:, pl.ds(base + t * mt, mt), :]

    def b_cols(u):
        return pl.ds((u % 2) * kw + (u // 2) * cw, cw)

    def b_slot(who, u):
        return b_land.at[:, pl.ds(pl.multiple_of(who * rows, rows), rows), b_cols(u)]

    def right_copy(j, t):
        return remote(a_slot(j, t), a_slot(j, t), a_right.at[j, t], a_recv.at[j, t], {"col": col + 1})

    def left_copy(j, t):
        return remote(a_slot(j, t), a_slot(j, t), a_left.at[j, t], a_recv.at[j, t], {"col": col - 1})

    def ya_copy(t):
        return remote(a_rows(t, half), a_slot(col, t), ya_send.at[t], a_recv.at[col, t], partner)

    def yb_copy(u):
        return remote(
            x_ref.at[:, :, b_cols(u)], b_slot(row, u), yb_send.at[u], b_recv.at[0, u], partner
        )

    def b_copy(kind, u):
        who = row2 if kind == 2 else row
        device = {"row": row2} if kind == 1 else {"row": row1}
        return remote(
            b_slot(who, u), b_slot(who, u), b_send.at[kind, u], b_recv.at[kind + 1, u], device
        )

    def b_wait(kind, who, u):
        pltpu.make_async_copy(b_slot(who, u), b_slot(who, u), b_recv.at[kind, u]).wait()

    def convert(who, u):
        step = 64
        part = u % 2

        @pl.loop(0, rows // step)
        def _(i):
            at = pl.ds(pl.multiple_of(who * rows + i * step, step), step)
            hi, lo = split(b_land[:, at, b_cols(u)])
            b_hi[u // 2, :, at, part * cw:(part + 1) * cw] = hi
            b_lo[u // 2, :, at, part * cw:(part + 1) * cw] = lo

    def handle(j, t):
        pltpu.make_async_copy(a_slot(j, t), a_slot(j, t), a_recv.at[j, t]).wait()

        @pl.when(jnp.logical_and(j <= col, has_right))
        def _():
            right_copy(j, t).start()

        @pl.when(jnp.logical_and(j >= col, has_left))
        def _():
            left_copy(j, t).start()

    def a_tick(e):
        for count, sign in ((col, -1), (n_col - 1 - col, 1)):
            @pl.when(jnp.logical_and(e >= 0, e < T * count))
            def _():
                n = jnp.maximum(count, 1)
                t = lax.div(e, n)
                handle(col + sign * (e - t * n + 1), t)

    def load(j, t):
        for mat in range(2):
            for part in range(2):
                at = pl.ds((2 * mat + part) * mt, mt)
                hi, lo = split(a_land[j, t, mat, :, part * kw:(part + 1) * kw])
                lhs[at, 0:kw] = hi
                lhs[at, kw:2 * kw] = hi
                lhs[at, 2 * kw:3 * kw] = lo

    def add(j, v):
        deep = pl.ds(pl.multiple_of(j * kw, kw), kw)
        rhs = []
        for mat in range(2):
            hi, lo = b_hi[v, mat, deep, :], b_lo[v, mat, deep, :]
            rhs.append(jnp.concatenate([hi, lo, hi], axis=0))
        acc[v] += jnp.dot(lhs[...], rhs[0], preferred_element_type=jnp.float32)
        acc[v, 2 * mt:4 * mt, :] += jnp.dot(
            lhs[0:2 * mt, :], rhs[1], preferred_element_type=jnp.float32
        )

    def out_at(t, v, part, base):
        return o_ref.at[
            :, pl.ds(pl.multiple_of(base + t * mt, mt), mt),
            pl.ds(pl.multiple_of(part * kw + v * cw, cw), cw),
        ]

    def out_from(t, v, part):
        return out_v.at[t, :, :, pl.ds(pl.multiple_of(part * kw + v * cw, cw), cw)]

    def out_remote(t, v, part):
        return remote(
            out_from(t, v, part), out_at(t, v, part, parity * half),
            out_sem.at[0, t, v, part], out_sem.at[1, t, v, part], partner,
        )

    def out_local(t, v, part):
        return pltpu.make_async_copy(
            out_from(t, v, part), out_at(t, v, part, parity * half), out_sem.at[2, t, v, part]
        )

    def finish(t, v):
        for mat in range(2):
            p = acc[v, 2 * mat * mt:(2 * mat + 1) * mt, :]
            q = acc[v, (2 * mat + 1) * mt:(2 * mat + 2) * mt, :]
            re, im = (pl.ds(pl.multiple_of(part * kw + v * cw, cw), cw) for part in range(2))
            out_v[t, mat, :, re] = p[:, 0:cw] - q[:, cw:]
            out_v[t, mat, :, im] = p[:, cw:] + q[:, 0:cw]
        for part in range(2):
            out_local(t, v, part).start()

    def send(t, v):
        for part in range(2):
            out_remote(t, v, part).start()

    def clear(v0, v1):
        @pl.loop(v0, v1)
        def _(v):
            acc[v] = jnp.zeros((4 * mt, 2 * cw), jnp.float32)

    def sum_block(t, v0, v1, reach):
        @pl.loop(0, 2 * reach + 1)
        def _(i):
            j = col + lax.div(i + 1, 2) * (1 - 2 * lax.rem(i, 2))

            @pl.when(jnp.logical_and(j >= 0, j < n_col))
            def _():
                load(j, t)

                @pl.loop(v0, v1)
                def _(v):
                    add(j, v)

    def block(t, v0, v1, hold):
        clear(v0, v1)
        sum_block(t, v0, v1, n_col - 1)

        @pl.loop(v0, v1)
        def _(v):
            finish(t, v)
            if hold:
                @pl.when(parity == 0)
                def _():
                    send(t, v)
            else:
                send(t, v)

    barrier = pltpu.get_barrier_semaphore()
    for device in (partner, {"row": row1}, {"row": row2}):
        pl.semaphore_signal(barrier, inc=1, device_id=device, device_id_type=MESH)

    @pl.when(has_left)
    def _():
        pl.semaphore_signal(barrier, inc=1, device_id={"col": col - 1}, device_id_type=MESH)

    @pl.when(has_right)
    def _():
        pl.semaphore_signal(barrier, inc=1, device_id={"col": col + 1}, device_id_type=MESH)

    pl.semaphore_wait(barrier, 3 + has_left.astype(jnp.int32) + has_right.astype(jnp.int32))

    @pl.when(parity == 0)
    def _():
        for t in range(T):
            if t < 2:
                ya_copy(t).start()
            pltpu.make_async_copy(a_rows(t, 0), a_slot(col, t), a_recv.at[col, t]).start()

    @pl.when(parity == 1)
    def _():
        for u in range(U):
            if u < 3:
                yb_copy(u).start()
            pltpu.make_async_copy(
                x_ref.at[:, :, b_cols(u)], b_slot(row, u), b_recv.at[0, u]
            ).start()

    last = n_col - 1
    a_ticks = T * last

    def own_b(u):
        b_wait(0, row, u)
        b_copy(1, u).start()
        b_copy(0, u).start()

    @pl.when(parity == 1)
    def _():
        own_b(0)

    is_end = jnp.logical_or(col == 0, col == last)
    incoming = jnp.maximum(col, last - col)
    pace = jnp.minimum(col, last - col) + 1

    def ready(t):
        return (t + 1) * incoming - 1 + parity

    def done_at(t, tick):
        return jnp.where(ready(t) <= tick, min(max((tick - 1) // 2, 0), V), 0)

    for tick in range(max(a_ticks + 1, U + 2)):
        if tick < U:
            @pl.when(parity == 0)
            def _():
                own_b(tick)
        if tick + 1 < U:
            @pl.when(parity == 1)
            def _():
                own_b(tick + 1)
        for t in range(T):
            @pl.when(jnp.maximum(t * pace - 1 + parity, 0) == tick)
            def _():
                handle(col, t)
        if tick < a_ticks:
            e = tick - parity
            if tick == a_ticks - 1:
                e = jnp.where(parity == 0, -1, e)
            a_tick(e)
        if tick == a_ticks:
            a_tick(a_ticks - 1)
        if 1 <= tick < U + 1:
            b_wait(2, row2, tick - 1)
            b_copy(2, tick - 1).start()
        if tick + 3 < U:
            @pl.when(parity == 1)
            def _():
                yb_copy(tick).wait_send()
                yb_copy(tick + 3).start()
        if tick + 2 < T:
            @pl.when(parity == 0)
            def _():
                ya_copy(tick).wait_send()
                ya_copy(tick + 2).start()
        if tick < U:
            convert(row, tick)
        if 1 <= tick < U + 1:
            b_wait(1, row1, tick - 1)
            convert(row1, tick - 1)
            convert(row2, tick - 1)
        if 2 <= tick < U + 2:
            b_wait(3, row3, tick - 2)
            convert(row3, tick - 2)
        if tick == U:
            @pl.when(parity == 1)
            def _():
                for u in range(max(U - 3, 0), U):
                    yb_copy(u).wait_send()

                @pl.loop(0, T)
                def _(t):
                    @pl.loop(0, jnp.where(jnp.logical_and(is_end, t == T - 1), 0, done_at(t, tick - 1)))
                    def _(v):
                        send(t, v)

        if tick >= 3:
            @pl.loop(0, T - is_end.astype(jnp.int32))
            def _(t):
                v0, v1 = done_at(t, tick - 1), done_at(t, tick)

                @pl.when(v1 > v0)
                def _():
                    block(t, v0, v1, tick < U)

        if tick == max(a_ticks - 1, U + 1):
            @pl.when(is_end)
            def _():
                clear(0, V)
                sum_block(T - 1, 0, V, last - 1)

    @pl.when(is_end)
    def _():
        load(last - col, T - 1)

        @pl.loop(0, V)
        def _(v):
            add(last - col, v)
            finish(T - 1, v)
            send(T - 1, v)

    @pl.loop(0, T)
    def _(t):
        @pl.loop(0, V)
        def _(v):
            for part in range(2):
                out_local(t, v, part).wait()
                out_remote(t, v, part).wait_send()
                pltpu.make_async_copy(
                    out_from(t, v, part), out_at(t, v, part, (1 - parity) * half),
                    out_sem.at[1, t, v, part],
                ).wait()

    for kind in range(3):
        for u in range(U):
            b_copy(kind, u).wait_send()

    @pl.when(parity == 0)
    def _():
        for t in range(max(T - 2, 0), T):
            ya_copy(t).wait_send()

    @pl.loop(0, n_col)
    def _(j):
        @pl.when(jnp.logical_and(j <= col, has_right))
        def _():
            for t in range(T):
                right_copy(j, t).wait_send()

        @pl.when(jnp.logical_and(j >= col, has_left))
        def _():
            for t in range(T):
                left_copy(j, t).wait_send()


def shards(n_row, n_col, pairs):
    _, _, rows, width = pairs.shape
    T = ROW_CHUNKS
    U = width // LANES
    mt = rows // 2 // T
    dma = pltpu.SemaphoreType.DMA
    combined = pl.pallas_call(
        functools.partial(kernel, n_col),
        out_shape=jax.ShapeDtypeStruct((2, rows, width), jnp.float32),
        in_specs=[pl.BlockSpec(memory_space=pl.ANY)],
        out_specs=pl.BlockSpec(memory_space=pl.ANY),
        scratch_shapes=[
            pltpu.VMEM((n_col, T, 2, mt, width), jnp.float32),
            pltpu.VMEM((2, n_row * rows, width), jnp.float32),
            pltpu.VMEM((U // 2, 2, n_row * rows, 2 * LANES), jnp.bfloat16),
            pltpu.VMEM((U // 2, 2, n_row * rows, 2 * LANES), jnp.bfloat16),
            pltpu.VMEM((4 * mt, 3 * width // 2), jnp.bfloat16),
            pltpu.VMEM((U // 2, 4 * mt, 2 * LANES), jnp.float32),
            pltpu.VMEM((T, 2, mt, width), jnp.float32),
            dma((n_col, T)),
            dma((n_col, T)),
            dma((n_col, T)),
            dma((T,)),
            dma((4, U)),
            dma((U,)),
            dma((3, U)),
            dma((3, T, U // 2, 2)),
        ],
        compiler_params=pltpu.CompilerParams(
            collective_id=0, has_side_effects=True, vmem_limit_bytes=58 * 1024 * 1024
        ),
    )(pairs[0])
    return combined[None]


def solution(mesh):
    spec = P("sec", None, "row", "col")
    return jax.shard_map(
        functools.partial(shards, mesh.shape["row"], mesh.shape["col"]),
        mesh=mesh, in_specs=(spec,), out_specs=spec, check_vma=False,
    )
```

```python
import functools

import jax
import jax.numpy as jnp
from jax import lax
from jax.experimental import pallas as pl
from jax.experimental.pallas import tpu as pltpu
from jax.sharding import PartitionSpec as P

MESH = pl.DeviceIdType.MESH
ROW_CHUNKS = 4
LANES = 128


def split(x):
    hi = x.astype(jnp.bfloat16)
    lo = (x - hi.astype(jnp.float32)).astype(jnp.bfloat16)
    return hi, lo


def kernel(
    n_col, x_ref, o_ref, a_land, b_land, b_hi, b_lo, a_hi, a_lo, acc, out_v,
    a_recv, a_right, a_left, ya_send, b_recv, yb_send, b_send, out_sem,
):
    T = ROW_CHUNKS
    rows, width = x_ref.shape[1], x_ref.shape[2]
    U = width // LANES
    V = U // 2
    half = rows // 2
    mt = half // T
    kw = width // 2
    cw = LANES

    sec, row, col = lax.axis_index("sec"), lax.axis_index("row"), lax.axis_index("col")
    parity = lax.rem(sec, 2)
    partner = {"sec": sec + 1 - 2 * parity}
    row1 = row + 1 - 2 * lax.rem(row, 2)
    row2 = row + 2 - 4 * lax.rem(lax.div(row, 2), 2)
    row3 = row1 + row2 - row
    has_left, has_right = col > 0, col < n_col - 1

    def remote(src, dst, send, recv, device):
        return pltpu.make_async_remote_copy(
            src_ref=src, dst_ref=dst, send_sem=send, recv_sem=recv,
            device_id=device, device_id_type=MESH,
        )

    def a_slot(j, t):
        return a_land.at[j, t]

    def a_rows(t, base):
        return x_ref.at[:, pl.ds(base + t * mt, mt), :]

    def b_cols(u):
        return pl.ds((u % 2) * kw + (u // 2) * cw, cw)

    def b_slot(who, u):
        return b_land.at[:, pl.ds(pl.multiple_of(who * rows, rows), rows), b_cols(u)]

    def right_copy(j, t):
        return remote(a_slot(j, t), a_slot(j, t), a_right.at[j, t], a_recv.at[j, t], {"col": col + 1})

    def left_copy(j, t):
        return remote(a_slot(j, t), a_slot(j, t), a_left.at[j, t], a_recv.at[j, t], {"col": col - 1})

    def ya_copy(t):
        return remote(a_rows(t, half), a_slot(col, t), ya_send.at[t], a_recv.at[col, t], partner)

    def yb_copy(u):
        return remote(
            x_ref.at[:, :, b_cols(u)], b_slot(row, u), yb_send.at[u], b_recv.at[0, u], partner
        )

    def b_copy(kind, u):
        who = row2 if kind == 2 else row
        device = {"row": row2} if kind == 1 else {"row": row1}
        return remote(
            b_slot(who, u), b_slot(who, u), b_send.at[kind, u], b_recv.at[kind + 1, u], device
        )

    def b_wait(kind, who, u):
        pltpu.make_async_copy(b_slot(who, u), b_slot(who, u), b_recv.at[kind, u]).wait()

    def convert(who, u):
        step = 64
        part = u % 2

        @pl.loop(0, rows // step)
        def _(i):
            at = pl.ds(pl.multiple_of(who * rows + i * step, step), step)
            hi, lo = split(b_land[:, at, b_cols(u)])
            b_hi[u // 2, :, at, part * cw:(part + 1) * cw] = hi
            b_lo[u // 2, :, at, part * cw:(part + 1) * cw] = lo

    def handle(j, t):
        pltpu.make_async_copy(a_slot(j, t), a_slot(j, t), a_recv.at[j, t]).wait()

        @pl.when(jnp.logical_and(j <= col, has_right))
        def _():
            right_copy(j, t).start()

        @pl.when(jnp.logical_and(j >= col, has_left))
        def _():
            left_copy(j, t).start()

    def a_tick(e):
        for count, sign in ((col, -1), (n_col - 1 - col, 1)):
            @pl.when(jnp.logical_and(e >= 0, e < T * count))
            def _():
                n = jnp.maximum(count, 1)
                t = lax.div(e, n)
                handle(col + sign * (e - t * n + 1), t)

    def load(j, t):
        for mat in range(2):
            for part in range(2):
                at = pl.ds((2 * mat + part) * mt, mt)
                hi, lo = split(a_land[j, t, mat, :, part * kw:(part + 1) * kw])
                a_hi[j, t, at, :] = hi
                a_lo[j, t, at, :] = lo

    def add(j, t, v):
        deep = pl.ds(pl.multiple_of(j * kw, kw), kw)
        left_hi, left_lo = a_hi[j, t], a_lo[j, t]
        lhs = jnp.concatenate([left_hi, left_hi, left_lo], axis=1)
        rhs = []
        for mat in range(2):
            hi, lo = b_hi[v, mat, deep, :], b_lo[v, mat, deep, :]
            rhs.append(jnp.concatenate([hi, lo, hi], axis=0))
        acc[v] += jnp.dot(lhs, rhs[0], preferred_element_type=jnp.float32)
        acc[v, 2 * mt:4 * mt, :] += jnp.dot(
            lhs[0:2 * mt], rhs[1], preferred_element_type=jnp.float32
        )

    def out_at(t, v, part, base):
        return o_ref.at[
            :, pl.ds(pl.multiple_of(base + t * mt, mt), mt),
            pl.ds(pl.multiple_of(part * kw + v * cw, cw), cw),
        ]

    def out_from(t, v, part):
        return out_v.at[t, :, :, pl.ds(pl.multiple_of(part * kw + v * cw, cw), cw)]

    def out_remote(t, v, part):
        return remote(
            out_from(t, v, part), out_at(t, v, part, parity * half),
            out_sem.at[0, t, v, part], out_sem.at[1, t, v, part], partner,
        )

    def out_local(t, v, part):
        return pltpu.make_async_copy(
            out_from(t, v, part), out_at(t, v, part, parity * half), out_sem.at[2, t, v, part]
        )

    def finish(t, v):
        for mat in range(2):
            p = acc[v, 2 * mat * mt:(2 * mat + 1) * mt, :]
            q = acc[v, (2 * mat + 1) * mt:(2 * mat + 2) * mt, :]
            re, im = (pl.ds(pl.multiple_of(part * kw + v * cw, cw), cw) for part in range(2))
            out_v[t, mat, :, re] = p[:, 0:cw] - q[:, cw:]
            out_v[t, mat, :, im] = p[:, cw:] + q[:, 0:cw]
        for part in range(2):
            out_local(t, v, part).start()

    def send(t, v):
        for part in range(2):
            out_remote(t, v, part).start()

    def clear(v0, v1):
        @pl.loop(v0, v1)
        def _(v):
            acc[v] = jnp.zeros((4 * mt, 2 * cw), jnp.float32)

    def sum_block(t, v0, v1, reach):
        @pl.loop(0, 2 * reach + 1)
        def _(i):
            j = col + lax.div(i + 1, 2) * (1 - 2 * lax.rem(i, 2))

            @pl.when(jnp.logical_and(j >= 0, j < n_col))
            def _():
                @pl.when(v0 == 0)
                def _():
                    load(j, t)

                @pl.loop(v0, v1)
                def _(v):
                    add(j, t, v)

    def block(t, v0, v1, hold):
        clear(v0, v1)
        sum_block(t, v0, v1, n_col - 1)

        @pl.loop(v0, v1)
        def _(v):
            finish(t, v)
            if hold:
                @pl.when(parity == 0)
                def _():
                    send(t, v)
            else:
                send(t, v)

    barrier = pltpu.get_barrier_semaphore()
    for device in (partner, {"row": row1}, {"row": row2}):
        pl.semaphore_signal(barrier, inc=1, device_id=device, device_id_type=MESH)

    @pl.when(has_left)
    def _():
        pl.semaphore_signal(barrier, inc=1, device_id={"col": col - 1}, device_id_type=MESH)

    @pl.when(has_right)
    def _():
        pl.semaphore_signal(barrier, inc=1, device_id={"col": col + 1}, device_id_type=MESH)

    pl.semaphore_wait(barrier, 3 + has_left.astype(jnp.int32) + has_right.astype(jnp.int32))

    @pl.when(parity == 0)
    def _():
        for t in range(T):
            if t < 1:
                ya_copy(t).start()
            pltpu.make_async_copy(a_rows(t, 0), a_slot(col, t), a_recv.at[col, t]).start()

    @pl.when(parity == 1)
    def _():
        for u in range(U):
            if u < 3:
                yb_copy(u).start()
            pltpu.make_async_copy(
                x_ref.at[:, :, b_cols(u)], b_slot(row, u), b_recv.at[0, u]
            ).start()

    last = n_col - 1
    a_ticks = T * last

    def own_b(u):
        b_wait(0, row, u)
        b_copy(1, u).start()
        b_copy(0, u).start()

    @pl.when(parity == 1)
    def _():
        own_b(0)

    is_end = jnp.logical_or(col == 0, col == last)
    incoming = jnp.maximum(col, last - col)
    pace = jnp.minimum(col, last - col) + 1

    def ready(t):
        return (t + 1) * incoming - 1 + parity

    def done_at(t, tick):
        return jnp.where(ready(t) <= tick, min(max((tick - 1) // 2, 0), V), 0)

    for tick in range(max(a_ticks + 1, U + 2)):
        if tick < U:
            @pl.when(parity == 0)
            def _():
                own_b(tick)
        if tick + 1 < U:
            @pl.when(parity == 1)
            def _():
                own_b(tick + 1)
        own_t = lax.div(tick, pace)

        @pl.when(jnp.logical_and(own_t * pace == tick, own_t < T))
        def _():
            handle(col, own_t)

        if tick < a_ticks:
            e = tick - parity
            if tick == a_ticks - 1:
                e = jnp.where(parity == 0, -1, e)
            a_tick(e)
        if tick == a_ticks:
            a_tick(a_ticks - 1)
        if 1 <= tick < U + 1:
            b_wait(2, row2, tick - 1)
            b_copy(2, tick - 1).start()
        if tick + 3 < U:
            @pl.when(parity == 1)
            def _():
                yb_copy(tick).wait_send()
                yb_copy(tick + 3).start()
        if tick + 1 < T:
            @pl.when(parity == 0)
            def _():
                ya_copy(tick).wait_send()
                ya_copy(tick + 1).start()
        if tick < U:
            convert(row, tick)
        if 1 <= tick < U + 1:
            b_wait(1, row1, tick - 1)
            convert(row1, tick - 1)
            convert(row2, tick - 1)
        if 2 <= tick < U + 2:
            b_wait(3, row3, tick - 2)
            convert(row3, tick - 2)
        if tick == U:
            @pl.when(parity == 1)
            def _():
                for u in range(max(U - 3, 0), U):
                    yb_copy(u).wait_send()

                @pl.loop(0, T)
                def _(t):
                    @pl.loop(0, jnp.where(jnp.logical_and(is_end, t == T - 1), 0, done_at(t, tick - 1)))
                    def _(v):
                        send(t, v)

        if tick >= 3:
            @pl.loop(0, T - is_end.astype(jnp.int32))
            def _(t):
                v0, v1 = done_at(t, tick - 1), done_at(t, tick)

                @pl.when(v1 > v0)
                def _():
                    block(t, v0, v1, tick < U)

        if tick == max(a_ticks - 1, U + 1):
            @pl.when(is_end)
            def _():
                clear(0, V)
                sum_block(T - 1, 0, V, last - 1)

    @pl.when(is_end)
    def _():
        load(last - col, T - 1)

        @pl.loop(0, V)
        def _(v):
            add(last - col, T - 1, v)
            finish(T - 1, v)
            send(T - 1, v)

    @pl.loop(0, T)
    def _(t):
        @pl.loop(0, V)
        def _(v):
            for part in range(2):
                out_local(t, v, part).wait()
                out_remote(t, v, part).wait_send()
                pltpu.make_async_copy(
                    out_from(t, v, part), out_at(t, v, part, (1 - parity) * half),
                    out_sem.at[1, t, v, part],
                ).wait()

    for kind in range(3):
        for u in range(U):
            b_copy(kind, u).wait_send()

    @pl.when(parity == 0)
    def _():
        ya_copy(T - 1).wait_send()

    @pl.loop(0, n_col)
    def _(j):
        @pl.when(jnp.logical_and(j <= col, has_right))
        def _():
            for t in range(T):
                right_copy(j, t).wait_send()

        @pl.when(jnp.logical_and(j >= col, has_left))
        def _():
            for t in range(T):
                left_copy(j, t).wait_send()


def shards(n_row, n_col, pairs):
    _, _, rows, width = pairs.shape
    T = ROW_CHUNKS
    U = width // LANES
    mt = rows // 2 // T
    dma = pltpu.SemaphoreType.DMA
    combined = pl.pallas_call(
        functools.partial(kernel, n_col),
        out_shape=jax.ShapeDtypeStruct((2, rows, width), jnp.float32),
        in_specs=[pl.BlockSpec(memory_space=pl.ANY)],
        out_specs=pl.BlockSpec(memory_space=pl.ANY),
        scratch_shapes=[
            pltpu.VMEM((n_col, T, 2, mt, width), jnp.float32),
            pltpu.VMEM((2, n_row * rows, width), jnp.float32),
            pltpu.VMEM((U // 2, 2, n_row * rows, 2 * LANES), jnp.bfloat16),
            pltpu.VMEM((U // 2, 2, n_row * rows, 2 * LANES), jnp.bfloat16),
            pltpu.VMEM((n_col, T, 4 * mt, width // 2), jnp.bfloat16),
            pltpu.VMEM((n_col, T, 4 * mt, width // 2), jnp.bfloat16),
            pltpu.VMEM((U // 2, 4 * mt, 2 * LANES), jnp.float32),
            pltpu.VMEM((T, 2, mt, width), jnp.float32),
            dma((n_col, T)),
            dma((n_col, T)),
            dma((n_col, T)),
            dma((T,)),
            dma((4, U)),
            dma((U,)),
            dma((3, U)),
            dma((3, T, U // 2, 2)),
        ],
        compiler_params=pltpu.CompilerParams(
            collective_id=0, has_side_effects=True, vmem_limit_bytes=58 * 1024 * 1024
        ),
    )(pairs[0])
    return combined[None]


def solution(mesh):
    spec = P("sec", None, "row", "col")
    return jax.shard_map(
        functools.partial(shards, mesh.shape["row"], mesh.shape["col"]),
        mesh=mesh, in_specs=(spec,), out_specs=spec, check_vma=False,
    )
```
